512 devices in a mesh: dp: 32 (over x_hi, y, core), ctx: 16 (over z, x_lo).
Axes of the slice: x: 4 (x_hi: 2, x_lo: 2; x = x_hi * 2 + x_lo), y: 8, z: 8, core: 2. Of those that a mesh axis runs over, the one named last changes fastest.
Arguments:
- inputs: bfloat16 [65536, 8192], P(('dp', 'ctx')), may hold values from -8 to 8
- key_output_gradient: bfloat16 [65536, 640], P(('dp', 'ctx')), may hold values from -240 to 240
- frozen_key_weight: bfloat16 [8192, 640], P('dp'), may hold values from -0.0625 to 0.0625
- adapter_first_factor: bfloat16 [8192, 64], P('dp'), may hold values from -0.0625 to 0.0625
- adapter_second_factor: bfloat16 [64, 640], replicated, may hold values from -0.75 to 0.75
- privacy_noise_first: float32 [8192, 64], P('ctx'), may hold values from -6 to 6
- privacy_noise_second: float32 [64, 640], P(None, 'ctx'), may hold values from -6 to 6
Outputs:
- d_input: bfloat16 [65536, 8192], P(('dp', 'ctx'))
- grad_a: float32 [8192, 64], P('ctx')
- grad_b: float32 [64, 640], P(None, 'ctx')
The draws below stay inside these ranges and needn't reach their ends.
All inputs are finite; a program needn't handle non-finite values.
Results may differ from the reference program's by a relative error of at most 0.014.
Values may be sent and summed in bfloat16 or wider, within the bound.
No kernel may reach another device: no remote copies, remote signals or barrier semaphores. Data moves between devices by JAX's collectives and lax.ppermute only.
A program may use at most 64 MiB of HBM per device.

```python
import math
import jax
import jax.numpy as jnp
from jax import lax

MODEL_WIDTH = 8192
KEY_FEATURES = 640
ADAPTER_RANK = 64
DOC_TOK = 2048
TOKENS = 65536
N_DP = 32


def shared_directions(key):
    input_key, output_key, strength_key = jax.random.split(key, 3)
    input_dirs = jnp.clip(jax.random.normal(input_key, (N_DP, MODEL_WIDTH), jnp.float32), -4.0, 4.0)
    output_dirs = jnp.clip(jax.random.normal(output_key, (N_DP, KEY_FEATURES), jnp.float32), -4.0, 4.0)
    ratio = jnp.exp(jax.random.uniform(strength_key, (N_DP,), jnp.float32, math.log(0.3), math.log(12.0)))
    strength = jnp.sqrt(jnp.minimum(ratio / math.sqrt(DOC_TOK), 1.0))
    input_rows = jnp.repeat(input_dirs * strength[:, None], DOC_TOK, axis=0, total_repeat_length=TOKENS)
    output_rows = jnp.repeat(output_dirs * strength[:, None], DOC_TOK, axis=0, total_repeat_length=TOKENS)
    return (input_rows, output_rows)


def draw_inputs(key, part):
    input_rows, output_rows = shared_directions(key)
    key = jax.random.fold_in(key, 11)
    base = jnp.clip(jax.random.normal(key, (TOKENS, MODEL_WIDTH), jnp.float32), -4.0, 4.0)
    return (base + input_rows).astype(jnp.bfloat16)


def draw_key_output_gradient(key, part):
    input_rows, output_rows = shared_directions(key)
    key = jax.random.fold_in(key, 7)
    base_key, doc_key, row_key = jax.random.split(key, 3)
    doc_scale = jnp.exp(jax.random.uniform(doc_key, (N_DP,), jnp.float32, math.log(0.5), math.log(5.0)))
    row_scale = jnp.exp(jax.random.uniform(row_key, (TOKENS,), jnp.float32, math.log(0.5), math.log(2.0)))
    position = (jnp.arange(TOKENS) % DOC_TOK).astype(jnp.float32)
    rising = jnp.exp(math.log(3.0) * position / DOC_TOK)
    scales = jnp.repeat(doc_scale, DOC_TOK, total_repeat_length=TOKENS) * row_scale * rising
    base = jnp.clip(jax.random.normal(base_key, (TOKENS, KEY_FEATURES), jnp.float32), -4.0, 4.0)
    return ((base + output_rows) * scales[:, None]).astype(jnp.bfloat16)


def level_of(own_key, extent, cuts, smallest, high):
    def one(axis_at, parts):
        steps = jax.random.uniform(jax.random.fold_in(jax.random.fold_in(own_key, 6), axis_at), (parts,), jnp.float32, smallest / len(cuts), high / len(cuts))
        return jnp.repeat(jnp.exp(steps), extent[axis_at] // parts).reshape((-1,) + (1,) * (len(extent) - axis_at - 1))

    factor_of = one(*cuts[0])
    for cut in cuts[1:]:
        factor_of = factor_of * one(*cut)
    return factor_of


def gaussian(rng, extent, width, limit, shards=(), held_as=jnp.bfloat16):
    array = width * jax.random.normal(rng, extent, jnp.float32)
    if shards:
        array = array * level_of(rng, extent, shards, -0.22, 0.18)
    return jnp.clip(array, -limit, limit).astype(held_as)


def setup_inputs(seed: int = 0) -> dict:
    keys = jax.random.split(jax.random.key(seed), 8)
    inputs = draw_inputs(jax.random.fold_in(keys[7], 71), 0)
    key_output_gradient = draw_key_output_gradient(jax.random.fold_in(keys[7], 71), 0)
    frozen_key_weight = gaussian(keys[2], (MODEL_WIDTH, KEY_FEATURES), MODEL_WIDTH ** -0.5, 0.0625, ((0, 32),))
    adapter_first_factor = gaussian(keys[3], (MODEL_WIDTH, ADAPTER_RANK), MODEL_WIDTH ** -0.5, 0.0625, ((0, 32),))
    adapter_second_factor = gaussian(keys[4], (ADAPTER_RANK, KEY_FEATURES), ADAPTER_RANK ** -0.5, 0.75)
    privacy_noise_first = gaussian(keys[5], (MODEL_WIDTH, ADAPTER_RANK), 1.0, 6.0, ((0, 16),), jnp.float32)
    privacy_noise_second = gaussian(keys[6], (ADAPTER_RANK, KEY_FEATURES), 1.0, 6.0, ((1, 16),), jnp.float32)
    return dict(inputs=inputs, key_output_gradient=key_output_gradient, frozen_key_weight=frozen_key_weight, adapter_first_factor=adapter_first_factor, adapter_second_factor=adapter_second_factor, privacy_noise_first=privacy_noise_first, privacy_noise_second=privacy_noise_second)


ADAPTER_SCALE = 2.0
NOISE = 0.005

def reference(inputs, key_output_gradient, frozen_key_weight, adapter_first_factor, adapter_second_factor, privacy_noise_first, privacy_noise_second):
    docs = N_DP
    doc_x = inputs.reshape(docs, DOC_TOK, MODEL_WIDTH)
    doc_g = key_output_gradient.reshape(docs, DOC_TOK, KEY_FEATURES)

    def per_doc(pair):
        document_input, document_output_gradient = pair
        lowrank_gradient = (ADAPTER_SCALE * jnp.dot(document_output_gradient, adapter_second_factor.T, preferred_element_type=jnp.float32)).astype(jnp.bfloat16)
        hidden_lowrank = jnp.dot(document_input, adapter_first_factor, preferred_element_type=jnp.float32).astype(jnp.bfloat16)
        document_input_gradient = (jnp.dot(document_output_gradient, frozen_key_weight.T, preferred_element_type=jnp.float32) + jnp.dot(lowrank_gradient, adapter_first_factor.T, preferred_element_type=jnp.float32)).astype(jnp.bfloat16)
        grad_doc_a = jnp.dot(document_input.T, lowrank_gradient, preferred_element_type=jnp.float32)
        grad_doc_b = ADAPTER_SCALE * jnp.dot(hidden_lowrank.T, document_output_gradient, preferred_element_type=jnp.float32)
        return (document_input_gradient, grad_doc_a, grad_doc_b)
    d_docs, all_a, all_b = lax.map(per_doc, (doc_x, doc_g))
    norms = jnp.sqrt(lax.optimization_barrier(jnp.sum(all_a * all_a, axis=(1, 2))) + lax.optimization_barrier(jnp.sum(all_b * all_b, axis=(1, 2))))
    bound = jnp.mean(norms)
    factor = bound / jnp.maximum(norms, bound)
    sum_a = lax.optimization_barrier(jnp.sum(factor[:, None, None] * all_a, axis=0))
    sum_b = lax.optimization_barrier(jnp.sum(factor[:, None, None] * all_b, axis=0))
    grad_a = (sum_a + NOISE * bound * privacy_noise_first) / docs
    grad_b = (sum_b + NOISE * bound * privacy_noise_second) / docs
    return (d_docs.reshape(TOKENS, MODEL_WIDTH), grad_a, grad_b)
```

```python
import jax
import jax.numpy as jnp
from jax import lax
from jax.experimental import pallas as pl
from jax.experimental.pallas import tpu as pltpu
from jax.sharding import Mesh, PartitionSpec as P

ADAPTER_SCALE = 2.0
NOISE = 0.005
DOCS = 32
CTX = 16
BF16 = jnp.bfloat16
F32 = jnp.float32

PARTS = ("xh", "y", "core", "z", "xl")
PART_SIZES = (2, 8, 2, 8, 2)
DP_PARTS = ("xh", "y", "core")
CTX_PARTS = ("z", "xl")

NT = (((1,), (1,)), ((), ()))
NN = (((1,), (0,)), ((), ()))

SMEM = pl.BlockSpec(memory_space=pltpu.SMEM)
VMEM = pl.BlockSpec(memory_space=pltpu.VMEM)
ANY = pl.BlockSpec(memory_space=pl.ANY)


def dot(a, b, dims):
    return lax.dot_general(a, b, dims, preferred_element_type=F32)


def first_partials_kernel(place_ref, x_ref, g_ref, b_ref, keep_ref, send_ref, order_ref):
    order_ref[...] = jnp.zeros((8, 128), F32)
    u_t = (ADAPTER_SCALE * dot(b_ref[...], g_ref[...], NT)).astype(BF16)
    xl = place_ref[2]
    for ref, at in ((send_ref, 1 - xl), (keep_ref, xl)):
        for z in range(8):
            columns = pl.ds(pl.multiple_of((2 * z + at) * 512, 512), 512)
            ref[z] = dot(u_t, x_ref[:, columns], NN).astype(BF16)


def pair_sum_kernel(a_ref, b_ref, out_ref):
    out_ref[...] = (a_ref[...].astype(F32) + b_ref[...].astype(F32)).astype(BF16)


def second_partials_kernel(place_ref, x_ref, g_ref, own_ref, other_ref, order_ref, msg_ref, gbt_ref, z_ref):
    core = place_ref[0]
    h_t = jnp.zeros((64, 128), F32)
    for block in range(16):
        own_at = pl.multiple_of((2 * block + core) * 256, 256)
        other_at = pl.multiple_of((2 * block + 1 - core) * 256, 256)
        h_t += dot(own_ref[block], x_ref[:, pl.ds(own_at, 256)], NT)
        h_t += dot(other_ref[block], x_ref[:, pl.ds(other_at, 256)], NT)
    gbt_ref[...] = ADAPTER_SCALE * dot(g_ref[...].T, h_t.astype(BF16), NT)
    for q in range(8):
        z_ref[0:80, 64 * q : 64 * q + 64] = gbt_ref[pl.ds(q, 80, stride=8), :]
    z_ref[80:88, :] = jnp.zeros((8, 512), F32)
    keep = lax.broadcasted_iota(jnp.int32, (8, 512), 0) < 5
    for j in range(CTX):
        msg_ref[j] = jnp.where(keep, z_ref[5 * j : 5 * j + 8, :], 0.0).astype(BF16)


def document_share_kernel(first_ref, second_ref, out_ref):
    first = first_ref[0].astype(F32)
    for j in range(1, 8):
        first += first_ref[j].astype(F32)
    second = second_ref[0].astype(F32)
    for j in range(1, CTX):
        second += second_ref[j].astype(F32)
    square = jnp.sum(first * first, axis=0, keepdims=True) + jnp.sum(second * second, axis=0, keepdims=True)
    square = jnp.broadcast_to(jnp.sum(square, axis=1, keepdims=True), (8, 128))
    high = square.astype(BF16).astype(F32)
    middle = (square - high).astype(BF16).astype(F32)
    low = square - high - middle
    row = lax.broadcasted_iota(jnp.int32, (8, 128), 0)
    for k in range(DOCS):
        a, lane = k // 4, 128 * (k % 4)
        tail = jnp.where(row == 1, high, jnp.where(row == 2, middle, jnp.where(row == 3, low, 0.0)))
        tail = jnp.where(row == 0, second[a : a + 1, lane : lane + 128], tail)
        out_ref[k] = jnp.concatenate([first[8 * a : 8 * a + 8, lane : lane + 128], tail], axis=0).astype(BF16)


def squares_kernel(shares_ref, out_ref):
    rows = shares_ref[:, 9, :].astype(F32) + shares_ref[:, 10, :].astype(F32) + shares_ref[:, 11, :].astype(F32)
    group = lax.broadcasted_iota(jnp.int32, (8, 128), 1) // 32
    packed = rows[0:8]
    for at in range(1, 4):
        packed = jnp.where(group == at, rows[8 * at : 8 * at + 8], packed)
    for j in range(CTX):
        out_ref[j] = packed


def clipped_sum_kernel(shares_ref, squares_ref, out_ref):
    squares = squares_ref[0]
    for j in range(1, CTX):
        squares += squares_ref[j]
    norms = jnp.sqrt(
        jnp.concatenate([jnp.broadcast_to(squares[:, 32 * at : 32 * at + 1], (8, 128)) for at in range(4)], axis=0)
    )
    bound = jnp.sum(norms, axis=0, keepdims=True) / DOCS
    factor = bound / jnp.maximum(norms, bound)
    total = factor[0:1] * shares_ref[0].astype(F32)
    for k in range(1, DOCS):
        total += factor[k : k + 1] * shares_ref[k].astype(F32)
    row = lax.broadcasted_iota(jnp.int32, (16, 128), 0)
    total = jnp.where(row == 9, bound, total)
    for k in range(DOCS):
        out_ref[k] = total


def finish_kernel(tiles_ref, noise_a_ref, noise_b_ref, order_ref, grad_a_ref, grad_b_ref, z_ref):
    noise = NOISE * tiles_ref[0, 9:10, 0:1]
    for k in range(DOCS):
        a, lane = 8 * (k // 4), 128 * (k % 4)
        grad_a_ref[a : a + 8, lane : lane + 128] = (
            tiles_ref[k, 0:8, :] + noise * noise_a_ref[a : a + 8, lane : lane + 128]
        ) / DOCS
        z_ref[k // 4 : k // 4 + 1, lane : lane + 128] = tiles_ref[k, 8:9, :]
    for q in range(8):
        at = pl.ds(q, 5, stride=8)
        grad_b_ref[at, :] = (z_ref[0:5, 64 * q : 64 * q + 64] + noise * noise_b_ref[at, :]) / DOCS


def input_gradient_kernel(place_ref, *refs):
    g_refs, (b_ref, at_ref), w_refs, out_refs = refs[0:4], refs[4:6], refs[6:14], refs[14:18]
    g = jnp.concatenate([ref[...] for ref in g_refs], axis=0)
    u = (ADAPTER_SCALE * dot(g, b_ref[...], NT)).astype(BF16)
    for back in range(8):
        y = (place_ref[3] + 8 - back) % 8
        out = (dot(g, w_refs[back][...], NT) + dot(u, at_ref[place_ref[1] * 8 + y], NN)).astype(BF16)
        for at, ref in enumerate(out_refs):
            ref[back] = out[128 * at : 128 * at + 128]


def interleave_kernel(place_ref, *refs):
    own_ref, core_ref, xh_ref, both_ref, out_ref = refs
    core, xh = place_ref[0], place_ref[1]
    for back in range(8):
        y = (place_ref[3] + 8 - back) % 8
        for ref, x_at, core_at in (
            (own_ref, xh, core),
            (core_ref, xh, 1 - core),
            (xh_ref, 1 - xh, core),
            (both_ref, 1 - xh, 1 - core),
        ):
            at = pl.multiple_of(((x_at * 8 + y) * 2 + core_at) * 256, 256)
            out_ref[:, pl.ds(at, 256)] = ref[back]


def exchange(pieces, axes):
    return lax.all_to_all(pieces, axes, 0, 0)


def swap(array, axes):
    count = 2 if isinstance(axes, str) else 4
    return lax.ppermute(array, axes, [(at, count - 1 - at) for at in range(count)])


def shift(array, by):
    return lax.ppermute(array, "y", [(at, (at + by) % 8) for at in range(8)])


def per_device(
    inputs,
    key_output_gradient,
    frozen_key_weight,
    adapter_first_factor,
    adapter_second_factor,
    privacy_noise_first,
    privacy_noise_second,
):
    place = jnp.stack([lax.axis_index(axis).astype(jnp.int32) for axis in ("core", "xh", "xl", "y")])

    factor_t = jnp.broadcast_to(adapter_first_factor.T[None], (16, 64, 256))
    factor_t = exchange(factor_t, ("xh", "y"))

    up, down = [frozen_key_weight], [frozen_key_weight]
    for _ in range(4):
        up.append(shift(up[-1], 1))
    for _ in range(3):
        down.append(shift(down[-1], 7))
    blocks = up + down[:0:-1]

    keep, send, order = pl.pallas_call(
        first_partials_kernel,
        in_specs=[SMEM] + [VMEM] * 3,
        out_shape=(jax.ShapeDtypeStruct((8, 64, 512), BF16),) * 2 + (jax.ShapeDtypeStruct((8, 128), F32),),
        name="first_partials",
    )(place, inputs, key_output_gradient, adapter_second_factor)
    first = pl.pallas_call(
        pair_sum_kernel, out_shape=jax.ShapeDtypeStruct((8, 64, 512), BF16), name="pair_sum"
    )(keep, swap(send, "xl"))
    first = exchange(first, "z")

    gradients = [key_output_gradient] + [swap(key_output_gradient, axes) for axes in ("core", "xh", ("xh", "core"))]

    second = pl.pallas_call(
        second_partials_kernel,
        in_specs=[SMEM] + [VMEM] * 4 + [ANY],
        out_shape=jax.ShapeDtypeStruct((CTX, 8, 512), BF16),
        scratch_shapes=[pltpu.VMEM((640, 64), F32), pltpu.VMEM((88, 512), F32)],
        name="second_partials",
    )(place, inputs, key_output_gradient, factor_t, swap(factor_t, "core"), order)
    second = exchange(second, CTX_PARTS)

    products = pl.pallas_call(
        input_gradient_kernel,
        in_specs=[SMEM] + [VMEM] * 14,
        out_shape=[jax.ShapeDtypeStruct((8, 128, 256), BF16)] * 4,
        compiler_params=pltpu.CompilerParams(vmem_limit_bytes=40 << 20),
        name="input_gradient",
    )(place, *gradients, adapter_second_factor, factor_t, *blocks)
    products = [products[0]] + [
        swap(product, axes) for product, axes in zip(products[1:], ("core", "xh", ("xh", "core")))
    ]
    d_input = pl.pallas_call(
        interleave_kernel,
        in_specs=[SMEM] + [VMEM] * 4,
        out_shape=jax.ShapeDtypeStruct((128, 8192), BF16),
        name="interleave",
    )(place, *products)

    shares = pl.pallas_call(
        document_share_kernel,
        out_shape=jax.ShapeDtypeStruct((DOCS, 16, 128), BF16),
        name="document_share",
    )(first, second)
    shares = exchange(shares, DP_PARTS)

    squares = pl.pallas_call(
        squares_kernel,
        out_shape=jax.ShapeDtypeStruct((CTX, 8, 128), F32),
        name="squares",
    )(shares)
    squares = exchange(squares, CTX_PARTS)

    tiles = pl.pallas_call(
        clipped_sum_kernel,
        out_shape=jax.ShapeDtypeStruct((DOCS, 16, 128), F32),
        name="clipped_sum",
    )(shares, squares)
    tiles = exchange(tiles, DP_PARTS)

    grad_a, grad_b = pl.pallas_call(
        finish_kernel,
        in_specs=[VMEM] * 3 + [ANY],
        out_shape=(jax.ShapeDtypeStruct((64, 512), F32), jax.ShapeDtypeStruct((40, 64), F32)),
        scratch_shapes=[pltpu.VMEM((8, 512), F32)],
        name="finish",
    )(tiles, privacy_noise_first.T, privacy_noise_second.T, d_input)
    return (d_input, grad_a.T, grad_b.T)


def solution(mesh):
    parts = Mesh(mesh.devices.reshape(PART_SIZES), PARTS)
    return jax.shard_map(
        per_device,
        mesh=parts,
        in_specs=(
            P(PARTS, None),
            P(PARTS, None),
            P(DP_PARTS, None),
            P(DP_PARTS, None),
            P(),
            P(CTX_PARTS, None),
            P(None, CTX_PARTS),
        ),
        out_specs=(P(PARTS, None), P(CTX_PARTS, None), P(None, CTX_PARTS)),
        check_vma=False,
    )
```

```python
import jax
import jax.numpy as jnp
from jax import lax
from jax.experimental import pallas as pl
from jax.experimental.pallas import tpu as pltpu
from jax.sharding import Mesh, PartitionSpec as P

ADAPTER_SCALE = 2.0
NOISE = 0.005
DOCS = 32
CTX = 16
BF16 = jnp.bfloat16
F32 = jnp.float32

PARTS = ("xh", "y", "core", "z", "xl")
PART_SIZES = (2, 8, 2, 8, 2)
DP_PARTS = ("xh", "y", "core")
CTX_PARTS = ("z", "xl")

NT = (((1,), (1,)), ((), ()))
NN = (((1,), (0,)), ((), ()))

VMEM_LIMIT = pltpu.CompilerParams(vmem_limit_bytes=24 << 20)
SMEM = pl.BlockSpec(memory_space=pltpu.SMEM)
VMEM = pl.BlockSpec(memory_space=pltpu.VMEM)
ANY = pl.BlockSpec(memory_space=pl.ANY)


def in_vmem(*arrays):
    return [pltpu.with_memory_space_constraint(array, pltpu.VMEM) for array in arrays]


def in_hbm(*arrays):
    return [pltpu.with_memory_space_constraint(array, pltpu.HBM) for array in arrays]


def dot(a, b, dims):
    return lax.dot_general(a, b, dims, preferred_element_type=F32)


def three_terms(value):
    high = value.astype(BF16).astype(F32)
    middle = (value - high).astype(BF16).astype(F32)
    return high, middle, value - high - middle


def copies_kernel(in_ref, out_ref):
    for at in range(16):
        out_ref[at] = in_ref[...]


def partials_kernel(place_ref, x_ref, g_ref, b_ref, own_ref, other_ref, *refs):
    msg_ref, gbt_ref, z_ref = refs[-3:]
    core = place_ref[0]
    g = g_ref[...]
    u_t = (ADAPTER_SCALE * dot(b_ref[...], g, NT)).astype(BF16)
    h_t = jnp.zeros((64, 128), F32)
    for block in range(16):
        own_at = pl.multiple_of((2 * block + core) * 256, 256)
        other_at = pl.multiple_of((2 * block + 1 - core) * 256, 256)
        h_t += dot(own_ref[block], x_ref[:, pl.ds(own_at, 256)], NT)
        h_t += dot(other_ref[block], x_ref[:, pl.ds(other_at, 256)], NT)
    for j in range(CTX):
        msg_ref[j, 0:64, :] = dot(u_t, x_ref[:, 512 * j : 512 * j + 512], NN).astype(BF16)
    gbt_ref[...] = ADAPTER_SCALE * dot(g.T, h_t.astype(BF16), NT)
    for q in range(8):
        z_ref[0:80, 64 * q : 64 * q + 64] = gbt_ref[pl.ds(q, 80, stride=8), :]
    z_ref[80:88, :] = jnp.zeros((8, 512), F32)
    keep = lax.broadcasted_iota(jnp.int32, (8, 512), 0) < 5
    for j in range(CTX):
        msg_ref[j, 64:72, :] = jnp.where(keep, z_ref[5 * j : 5 * j + 8, :], 0.0).astype(BF16)


def wait_kernel(*refs):
    pass


def document_share_kernel(parts_ref, up_ref, down_ref, share_ref, square_ref):
    total = parts_ref[0].astype(F32)
    for j in range(1, CTX):
        total += parts_ref[j].astype(F32)
    share_ref[...] = total
    square = jnp.sum(total * total, axis=0, keepdims=True)
    square = jnp.broadcast_to(jnp.sum(square, axis=1, keepdims=True), (8, 128))
    for j in range(CTX):
        square_ref[j] = square


def document_messages_kernel(share_ref, squares_ref, _, out_ref):
    square = squares_ref[0]
    for j in range(1, CTX):
        square += squares_ref[j]
    high, middle, low = three_terms(jnp.sqrt(square))
    row = lax.broadcasted_iota(jnp.int32, (8, 128), 0)
    norm = jnp.where(row == 1, high, jnp.where(row == 2, middle, jnp.where(row == 3, low, 0.0)))
    for k in range(DOCS):
        a, lane = k // 4, 128 * (k % 4)
        tail = jnp.where(row == 0, share_ref[64 + a : 65 + a, lane : lane + 128], norm)
        tile = share_ref[8 * a : 8 * a + 8, lane : lane + 128]
        out_ref[k] = jnp.concatenate([tile, tail], axis=0).astype(BF16)


def clipped_sum_kernel(messages_ref, out_ref):
    norms = messages_ref[:, 9, :].astype(F32) + messages_ref[:, 10, :].astype(F32) + messages_ref[:, 11, :].astype(F32)
    bound = jnp.sum(norms, axis=0, keepdims=True) / DOCS
    factor = bound / jnp.maximum(norms, bound)
    total = factor[0:1] * messages_ref[0].astype(F32)
    for k in range(1, DOCS):
        total += factor[k : k + 1] * messages_ref[k].astype(F32)
    high, middle, low = three_terms(bound)
    row = lax.broadcasted_iota(jnp.int32, (16, 128), 0)
    total = jnp.where(row == 9, high, jnp.where(row == 10, middle, jnp.where(row == 11, low, total))).astype(BF16)
    for k in range(DOCS):
        out_ref[k] = total


def finish_kernel(tiles_ref, noise_a_ref, noise_b_ref, _, grad_a_ref, grad_b_ref, z_ref):
    own = tiles_ref[0].astype(F32)
    noise = NOISE * (own[9:10, 0:1] + own[10:11, 0:1] + own[11:12, 0:1])
    for k in range(DOCS):
        a, lane = 8 * (k // 4), 128 * (k % 4)
        tile = tiles_ref[k].astype(F32)
        grad_a_ref[a : a + 8, lane : lane + 128] = (
            tile[0:8] + noise * noise_a_ref[a : a + 8, lane : lane + 128]
        ) / DOCS
        z_ref[k // 4 : k // 4 + 1, lane : lane + 128] = tile[8:9]
    for q in range(8):
        at = pl.ds(q, 5, stride=8)
        grad_b_ref[at, :] = (z_ref[0:5, 64 * q : 64 * q + 64] + noise * noise_b_ref[at, :]) / DOCS


def own_rows_kernel(place_ref, own_ref, other_ref, out_ref):
    out_ref[place_ref[1]] = own_ref[...]
    out_ref[1 - place_ref[1]] = other_ref[...]


def input_gradient_kernel(place_ref, *refs):
    g_refs, (b_ref, at_ref), w_refs, out_refs = refs[0:4], refs[4:6], refs[6:14], refs[14:18]
    g = jnp.concatenate([ref[...] for ref in g_refs], axis=0)
    u = (ADAPTER_SCALE * dot(g, b_ref[...], NT)).astype(BF16)
    half = pl.ds(pl.multiple_of(place_ref[2] * 128, 128), 128)
    for back in range(8):
        y = (place_ref[3] + 8 - back) % 8
        for xh in range(2):
            out = (dot(g, w_refs[back][xh], NT) + dot(u, at_ref[xh * 8 + y, :, half], NN)).astype(BF16)
            for at, ref in enumerate(out_refs):
                ref[back, :, 128 * xh : 128 * xh + 128] = out[128 * at : 128 * at + 128]


def interleave_kernel(place_ref, *refs):
    own_ref, core_ref, xl_ref, both_ref, out_ref = refs
    core, xl = place_ref[0], place_ref[2]
    for back in range(8):
        y = (place_ref[3] + 8 - back) % 8
        for ref, xl_at, core_at in (
            (own_ref, xl, core),
            (core_ref, xl, 1 - core),
            (xl_ref, 1 - xl, core),
            (both_ref, 1 - xl, 1 - core),
        ):
            for xh in range(2):
                at = pl.multiple_of((((xh * 8 + y) * 2 + core_at) * 2 + xl_at) * 128, 128)
                out_ref[:, pl.ds(at, 128)] = ref[back, :, 128 * xh : 128 * xh + 128]


def exchange(pieces, axes):
    return lax.all_to_all(pieces, axes, 0, 0)


def swap(array, axes):
    count = 2 if isinstance(axes, str) else 4
    return lax.ppermute(array, axes, [(at, count - 1 - at) for at in range(count)])


def shift(array, axis, by):
    return lax.ppermute(array, axis, [(at, (at + by) % 8) for at in range(8)])


def per_device(
    inputs,
    key_output_gradient,
    frozen_key_weight,
    adapter_first_factor,
    adapter_second_factor,
    privacy_noise_first,
    privacy_noise_second,
):
    place = jnp.stack([lax.axis_index(axis).astype(jnp.int32) for axis in ("core", "xh", "xl", "y", "z")])

    factor_t = pl.pallas_call(
        copies_kernel,
        in_specs=[VMEM],
        out_shape=pltpu.VMEM((16, 64, 256), BF16),
        compiler_params=VMEM_LIMIT,
        name="copies",
    )(adapter_first_factor.T)
    factor_t = exchange(factor_t, ("xh", "y"))

    gradients = [swap(key_output_gradient, axes) for axes in ("core", "xl", ("core", "xl"))]
    half = lax.dynamic_slice_in_dim(frozen_key_weight, place[2] * 128, 128, 0)
    near = pl.pallas_call(
        own_rows_kernel,
        in_specs=[SMEM] + [VMEM] * 2,
        out_shape=pltpu.VMEM((2, 128, 640), BF16),
        compiler_params=VMEM_LIMIT,
        name="own_rows",
    )(place, *in_vmem(half, swap(half, "xh")))
    factor_t = pl.pallas_call(
        wait_kernel,
        in_specs=[VMEM] * 5,
        out_shape=pltpu.VMEM(factor_t.shape, BF16),
        input_output_aliases={0: 0},
        compiler_params=VMEM_LIMIT,
        name="wait",
    )(*in_vmem(factor_t, near, *gradients))
    parts = pl.pallas_call(
        partials_kernel,
        in_specs=[SMEM] + [VMEM] * 5,
        out_shape=pltpu.VMEM((CTX, 72, 512), BF16),
        scratch_shapes=[pltpu.VMEM((640, 64), F32), pltpu.VMEM((88, 512), F32)],
        compiler_params=VMEM_LIMIT,
        name="partials",
    )(
        place,
        *in_hbm(inputs, key_output_gradient, adapter_second_factor),
        *in_vmem(factor_t, swap(factor_t, "core")),
    )
    parts = exchange(parts, CTX_PARTS)

    up1, down1 = in_hbm(shift(near, "y", 1), shift(near, "y", 7))
    up2, down2 = in_hbm(shift(up1, "y", 1), shift(down1, "y", 7))
    up3, down3 = in_hbm(shift(up2, "y", 1), shift(down2, "y", 7))
    (up4,) = in_hbm(shift(up3, "y", 1))
    blocks = [near, up1, up2, up3, up4, down3, down2, down1]
    share, squares = pl.pallas_call(
        document_share_kernel,
        in_specs=[VMEM, ANY, ANY],
        out_shape=(pltpu.VMEM((72, 512), F32), pltpu.VMEM((CTX, 8, 128), F32)),
        compiler_params=VMEM_LIMIT,
        name="document_share",
    )(*in_vmem(parts), *in_hbm(up3, down3))
    squares = exchange(squares, CTX_PARTS)

    products = pl.pallas_call(
        input_gradient_kernel,
        in_specs=[SMEM] + [VMEM] * 14,
        out_shape=[jax.ShapeDtypeStruct((8, 128, 256), BF16)] * 4,
        compiler_params=VMEM_LIMIT,
        name="input_gradient",
    )(place, key_output_gradient, *in_vmem(*gradients), adapter_second_factor, *in_vmem(factor_t, near), *in_hbm(*blocks[1:]))
    own = products[0]
    products = [own] + [
        swap(product, axes) for product, axes in zip(products[1:], ("core", "xl", ("core", "xl")))
    ]
    d_input = pl.pallas_call(
        interleave_kernel,
        in_specs=[SMEM] + [VMEM] * 4,
        out_shape=pltpu.HBM((128, 8192), BF16),
        compiler_params=VMEM_LIMIT,
        name="interleave",
    )(place, products[0], *in_vmem(*products[1:]))

    messages = pl.pallas_call(
        document_messages_kernel,
        in_specs=[VMEM, VMEM, ANY],
        out_shape=pltpu.VMEM((DOCS, 16, 128), BF16),
        compiler_params=VMEM_LIMIT,
        name="document_messages",
    )(*in_vmem(share, squares), own)
    messages = exchange(messages, DP_PARTS)

    tiles = pl.pallas_call(
        clipped_sum_kernel,
        in_specs=[VMEM],
        out_shape=pltpu.VMEM((DOCS, 16, 128), BF16),
        compiler_params=VMEM_LIMIT,
        name="clipped_sum",
    )(*in_vmem(messages))
    tiles = exchange(tiles, DP_PARTS)

    grad_a, grad_b = pl.pallas_call(
        finish_kernel,
        in_specs=[VMEM] * 3 + [ANY],
        out_shape=(jax.ShapeDtypeStruct((64, 512), F32), jax.ShapeDtypeStruct((40, 64), F32)),
        scratch_shapes=[pltpu.VMEM((8, 512), F32)],
        compiler_params=VMEM_LIMIT,
        name="finish",
    )(*in_vmem(tiles, privacy_noise_first.T, privacy_noise_second.T), *in_hbm(d_input))
    return (d_input, grad_a.T, grad_b.T)


def solution(mesh):
    parts = Mesh(mesh.devices.reshape(PART_SIZES), PARTS)
    return jax.shard_map(
        per_device,
        mesh=parts,
        in_specs=(
            P(PARTS, None),
            P(PARTS, None),
            P(DP_PARTS, None),
            P(DP_PARTS, None),
            P(),
            P(CTX_PARTS, None),
            P(None, CTX_PARTS),
        ),
        out_specs=(P(PARTS, None), P(CTX_PARTS, None), P(None, CTX_PARTS)),
        check_vma=False,
    )
```

```python
import jax
import jax.numpy as jnp
from jax import lax
from jax.experimental import pallas as pl
from jax.experimental.pallas import tpu as pltpu
from jax.sharding import Mesh, PartitionSpec as P

ADAPTER_SCALE = 2.0
NOISE = 0.005
DOCS = 32
CTX = 16
BF16 = jnp.bfloat16
F32 = jnp.float32

PARTS = ("xh", "y", "core", "z", "xl")
PART_SIZES = (2, 8, 2, 8, 2)
DP_PARTS = ("xh", "y", "core")
CTX_PARTS = ("z", "xl")

NT = (((1,), (1,)), ((), ()))
NN = (((1,), (0,)), ((), ()))

VMEM_LIMIT = pltpu.CompilerParams(vmem_limit_bytes=24 << 20)
SMEM = pl.BlockSpec(memory_space=pltpu.SMEM)
VMEM = pl.BlockSpec(memory_space=pltpu.VMEM)
ANY = pl.BlockSpec(memory_space=pl.ANY)


def in_vmem(*arrays):
    return [pltpu.with_memory_space_constraint(array, pltpu.VMEM) for array in arrays]


def in_hbm(*arrays):
    return [pltpu.with_memory_space_constraint(array, pltpu.HBM) for array in arrays]


def dot(a, b, dims):
    return lax.dot_general(a, b, dims, preferred_element_type=F32)


def three_terms(value):
    high = value.astype(BF16).astype(F32)
    middle = (value - high).astype(BF16).astype(F32)
    return high, middle, value - high - middle


def copies_kernel(in_ref, out_ref):
    for at in range(16):
        out_ref[at] = in_ref[...]


def partials_kernel(place_ref, x_ref, g_ref, b_ref, own_ref, other_ref, *refs):
    msg_ref, gbt_ref, z_ref = refs[-3:]
    core = place_ref[0]
    g = g_ref[...]
    u_t = (ADAPTER_SCALE * dot(b_ref[...], g, NT)).astype(BF16)
    h_t = jnp.zeros((64, 128), F32)
    for block in range(16):
        own_at = pl.multiple_of((2 * block + core) * 256, 256)
        other_at = pl.multiple_of((2 * block + 1 - core) * 256, 256)
        h_t += dot(own_ref[block], x_ref[:, pl.ds(own_at, 256)], NT)
        h_t += dot(other_ref[block], x_ref[:, pl.ds(other_at, 256)], NT)
    for j in range(CTX):
        msg_ref[j, 0:64, :] = dot(u_t, x_ref[:, 512 * j : 512 * j + 512], NN).astype(BF16)
    gbt_ref[...] = ADAPTER_SCALE * dot(g.T, h_t.astype(BF16), NT)
    for q in range(8):
        z_ref[0:80, 64 * q : 64 * q + 64] = gbt_ref[pl.ds(q, 80, stride=8), :]
    z_ref[80:88, :] = jnp.zeros((8, 512), F32)
    keep = lax.broadcasted_iota(jnp.int32, (8, 512), 0) < 5
    for j in range(CTX):
        msg_ref[j, 64:72, :] = jnp.where(keep, z_ref[5 * j : 5 * j + 8, :], 0.0).astype(BF16)


def wait_kernel(*refs):
    pass


def document_share_kernel(parts_ref, up_ref, down_ref, share_ref, square_ref):
    total = parts_ref[0].astype(F32)
    for j in range(1, CTX):
        total += parts_ref[j].astype(F32)
    share_ref[...] = total
    square = jnp.sum(total * total, axis=0, keepdims=True)
    square = jnp.broadcast_to(jnp.sum(square, axis=1, keepdims=True), (8, 128))
    for j in range(CTX):
        square_ref[j] = square


def document_messages_kernel(share_ref, squares_ref, out_ref):
    square = squares_ref[0]
    for j in range(1, CTX):
        square += squares_ref[j]
    high, middle, low = three_terms(jnp.sqrt(square))
    row = lax.broadcasted_iota(jnp.int32, (8, 128), 0)
    norm = jnp.where(row == 1, high, jnp.where(row == 2, middle, jnp.where(row == 3, low, 0.0)))
    for k in range(DOCS):
        a, lane = k // 4, 128 * (k % 4)
        tail = jnp.where(row == 0, share_ref[64 + a : 65 + a, lane : lane + 128], norm)
        tile = share_ref[8 * a : 8 * a + 8, lane : lane + 128]
        out_ref[k] = jnp.concatenate([tile, tail], axis=0).astype(BF16)


def clipped_sum_kernel(messages_ref, *refs):
    out_ref = refs[2]
    norms = messages_ref[:, 9, :].astype(F32) + messages_ref[:, 10, :].astype(F32) + messages_ref[:, 11, :].astype(F32)
    bound = jnp.sum(norms, axis=0, keepdims=True) / DOCS
    factor = bound / jnp.maximum(norms, bound)
    total = factor[0:1] * messages_ref[0].astype(F32)
    for k in range(1, DOCS):
        total += factor[k : k + 1] * messages_ref[k].astype(F32)
    high, middle, low = three_terms(bound)
    row = lax.broadcasted_iota(jnp.int32, (16, 128), 0)
    total = jnp.where(row == 9, high, jnp.where(row == 10, middle, jnp.where(row == 11, low, total))).astype(BF16)
    for k in range(DOCS):
        out_ref[k] = total


def finish_kernel(tiles_ref, noise_a_ref, noise_b_ref, _, grad_a_ref, grad_b_ref, z_ref):
    own = tiles_ref[0].astype(F32)
    noise = NOISE * (own[9:10, 0:1] + own[10:11, 0:1] + own[11:12, 0:1])
    for k in range(DOCS):
        a, lane = 8 * (k // 4), 128 * (k % 4)
        tile = tiles_ref[k].astype(F32)
        grad_a_ref[a : a + 8, lane : lane + 128] = (
            tile[0:8] + noise * noise_a_ref[a : a + 8, lane : lane + 128]
        ) / DOCS
        z_ref[k // 4 : k // 4 + 1, lane : lane + 128] = tile[8:9]
    for q in range(8):
        at = pl.ds(q, 5, stride=8)
        grad_b_ref[at, :] = (z_ref[0:5, 64 * q : 64 * q + 64] + noise * noise_b_ref[at, :]) / DOCS


def own_rows_kernel(place_ref, own_ref, other_ref, out_ref):
    out_ref[place_ref[1]] = own_ref[...]
    out_ref[1 - place_ref[1]] = other_ref[...]


def input_gradient_kernel(place_ref, *refs):
    g_refs, (b_ref, at_ref), w_refs, out_refs = refs[0:4], refs[4:6], refs[6:14], refs[14:18]
    g = jnp.concatenate([ref[...] for ref in g_refs], axis=0)
    u = (ADAPTER_SCALE * dot(g, b_ref[...], NT)).astype(BF16)
    half = pl.ds(pl.multiple_of(place_ref[2] * 128, 128), 128)
    for back in range(8):
        y = (place_ref[3] + 8 - back) % 8
        for xh in range(2):
            out = (dot(g, w_refs[back][xh], NT) + dot(u, at_ref[xh * 8 + y, :, half], NN)).astype(BF16)
            for at, ref in enumerate(out_refs):
                ref[back, :, 128 * xh : 128 * xh + 128] = out[128 * at : 128 * at + 128]


def interleave_kernel(place_ref, *refs):
    own_ref, core_ref, xl_ref, both_ref, out_ref = refs
    core, xl = place_ref[0], place_ref[2]
    for back in range(8):
        y = (place_ref[3] + 8 - back) % 8
        for ref, xl_at, core_at in (
            (own_ref, xl, core),
            (core_ref, xl, 1 - core),
            (xl_ref, 1 - xl, core),
            (both_ref, 1 - xl, 1 - core),
        ):
            for xh in range(2):
                at = pl.multiple_of((((xh * 8 + y) * 2 + core_at) * 2 + xl_at) * 128, 128)
                out_ref[:, pl.ds(at, 128)] = ref[back, :, 128 * xh : 128 * xh + 128]


def exchange(pieces, axes):
    return lax.all_to_all(pieces, axes, 0, 0)


def swap(array, axes):
    count = 2 if isinstance(axes, str) else 4
    return lax.ppermute(array, axes, [(at, count - 1 - at) for at in range(count)])


def shift(array, axis, by):
    return lax.ppermute(array, axis, [(at, (at + by) % 8) for at in range(8)])


def per_device(
    inputs,
    key_output_gradient,
    frozen_key_weight,
    adapter_first_factor,
    adapter_second_factor,
    privacy_noise_first,
    privacy_noise_second,
):
    place = jnp.stack([lax.axis_index(axis).astype(jnp.int32) for axis in ("core", "xh", "xl", "y", "z")])

    factor_t = pl.pallas_call(
        copies_kernel,
        in_specs=[VMEM],
        out_shape=pltpu.VMEM((16, 64, 256), BF16),
        compiler_params=VMEM_LIMIT,
        name="copies",
    )(*in_hbm(adapter_first_factor.T))
    factor_t = exchange(factor_t, ("xh", "y"))

    gradients = [swap(key_output_gradient, axes) for axes in ("core", "xl", ("core", "xl"))]
    half = lax.dynamic_slice_in_dim(frozen_key_weight, place[2] * 128, 128, 0)
    near = pl.pallas_call(
        own_rows_kernel,
        in_specs=[SMEM] + [VMEM] * 2,
        out_shape=pltpu.VMEM((2, 128, 640), BF16),
        compiler_params=VMEM_LIMIT,
        name="own_rows",
    )(place, *in_vmem(half, swap(half, "xh")))
    factor_t = pl.pallas_call(
        wait_kernel,
        in_specs=[VMEM] * 5,
        out_shape=pltpu.VMEM(factor_t.shape, BF16),
        input_output_aliases={0: 0},
        compiler_params=VMEM_LIMIT,
        name="wait",
    )(*in_vmem(factor_t, near, *gradients))
    parts = pl.pallas_call(
        partials_kernel,
        in_specs=[SMEM] + [VMEM] * 5,
        out_shape=pltpu.VMEM((CTX, 72, 512), BF16),
        scratch_shapes=[pltpu.VMEM((640, 64), F32), pltpu.VMEM((88, 512), F32)],
        compiler_params=VMEM_LIMIT,
        name="partials",
    )(
        place,
        *in_hbm(inputs, key_output_gradient, adapter_second_factor),
        *in_vmem(factor_t, swap(factor_t, "core")),
    )
    parts = exchange(parts, CTX_PARTS)

    up1, down1 = in_hbm(shift(near, "y", 1), shift(near, "y", 7))
    up2, down2 = in_hbm(shift(up1, "y", 1), shift(down1, "y", 7))
    up3, down3 = in_hbm(shift(up2, "y", 1), shift(down2, "y", 7))
    (up4,) = in_hbm(shift(up3, "y", 1))
    blocks = [near, up1, up2, up3, up4, down3, down2, down1]
    share, squares = pl.pallas_call(
        document_share_kernel,
        in_specs=[VMEM, ANY, ANY],
        out_shape=(pltpu.VMEM((72, 512), F32), pltpu.VMEM((CTX, 8, 128), F32)),
        compiler_params=VMEM_LIMIT,
        name="document_share",
    )(*in_vmem(parts), *in_hbm(up3, down3))
    squares = exchange(squares, CTX_PARTS)

    products = pl.pallas_call(
        input_gradient_kernel,
        in_specs=[SMEM] + [VMEM] * 14,
        out_shape=[pltpu.HBM((8, 128, 256), BF16)] * 4,
        compiler_params=VMEM_LIMIT,
        name="input_gradient",
    )(place, key_output_gradient, *in_vmem(*gradients), adapter_second_factor, *in_vmem(factor_t, near), *in_hbm(*blocks[1:]))
    xl_product = swap(products[2], "xl")
    messages = pl.pallas_call(
        document_messages_kernel,
        in_specs=[VMEM] * 2,
        out_shape=pltpu.VMEM((DOCS, 16, 128), BF16),
        compiler_params=VMEM_LIMIT,
        name="document_messages",
    )(*in_vmem(share, squares))
    messages = exchange(messages, DP_PARTS)

    tiles, *theirs = pl.pallas_call(
        clipped_sum_kernel,
        in_specs=[VMEM] + [ANY] * 2,
        out_specs=[VMEM] + [ANY] * 2,
        out_shape=[pltpu.VMEM((DOCS, 16, 128), BF16)] + [pltpu.HBM((8, 128, 256), BF16)] * 2,
        input_output_aliases={1: 1, 2: 2},
        compiler_params=VMEM_LIMIT,
        name="clipped_sum",
    )(*in_vmem(messages), *in_hbm(products[1], products[3]))
    products = [products[0], swap(theirs[0], "core"), xl_product, swap(theirs[1], ("core", "xl"))]
    d_input = pl.pallas_call(
        interleave_kernel,
        in_specs=[SMEM] + [VMEM] * 4,
        out_shape=pltpu.HBM((128, 8192), BF16),
        compiler_params=VMEM_LIMIT,
        name="interleave",
    )(place, *in_hbm(products[0]), *in_vmem(*products[1:]))

    tiles = exchange(tiles, DP_PARTS)

    grad_a, grad_b = pl.pallas_call(
        finish_kernel,
        in_specs=[VMEM] * 3 + [ANY],
        out_shape=(jax.ShapeDtypeStruct((64, 512), F32), jax.ShapeDtypeStruct((40, 64), F32)),
        scratch_shapes=[pltpu.VMEM((8, 512), F32)],
        compiler_params=VMEM_LIMIT,
        name="finish",
    )(*in_vmem(tiles, privacy_noise_first.T, privacy_noise_second.T), *in_hbm(d_input))
    return (d_input, grad_a.T, grad_b.T)


def solution(mesh):
    parts = Mesh(mesh.devices.reshape(PART_SIZES), PARTS)
    return jax.shard_map(
        per_device,
        mesh=parts,
        in_specs=(
            P(PARTS, None),
            P(PARTS, None),
            P(DP_PARTS, None),
            P(DP_PARTS, None),
            P(),
            P(CTX_PARTS, None),
            P(None, CTX_PARTS),
        ),
        out_specs=(P(PARTS, None), P(CTX_PARTS, None), P(None, CTX_PARTS)),
        check_vma=False,
    )
```
